256 devices in a mesh: cuts: 16 (over z, y_hi), loop: 16 (over y_lo, x, core).
Axes of the slice: x: 4, y: 4 (y_hi: 2, y_lo: 2; y = y_hi * 2 + y_lo), z: 8, core: 2. Of those that a mesh axis runs over, the one named last changes fastest.
Arguments:
- image_features: bfloat16 [65536, 1152], P(('cuts', 'loop')), may hold values from -0.1796875 to 0.1796875
- text_features: bfloat16 [65536, 1152], P(('cuts', 'loop')), may hold values from -0.1796875 to 0.1796875
- image_head: bfloat16 [1152, 1152], replicated, may hold values from -0.1875 to 0.1875
- text_head: bfloat16 [1152, 1152], replicated, may hold values from -0.1875 to 0.1875
Outputs:
- image_grad: float32 [65536, 1152], P(('cuts', 'loop'))
- text_grad: float32 [65536, 1152], P(('cuts', 'loop'))
- image_head_grad: float32 [1152, 1152], P('loop')
- text_head_grad: float32 [1152, 1152], P('loop')
The draws below stay inside these ranges and needn't reach their ends.
All inputs are finite; a program needn't handle non-finite values.
Results may differ from the reference program's by a relative error of at most 0.024.
Values may be sent and summed in bfloat16 or wider, within the bound.
A program may use at most 128 MiB of HBM per device.

```python
import jax
import jax.numpy as jnp
from jax import lax

D = 1152
B = 256
ROWS = 65536
N_CUTS = 16
N_LOOP = 16


def steps_of(rng, extent, split, low, high):
    level, own = 1.0, jax.random.fold_in(rng, 6)
    for position, blocks in split:
        heights = jnp.exp(jax.random.uniform(jax.random.fold_in(own, position), (blocks,), jnp.float32, low / len(split), high / len(split)))
        level = level * jnp.repeat(heights, extent[position] // blocks).reshape([-1 if axis == position else 1 for axis in range(len(extent))])
    return level


def gaussian(own_key, extent, scale, bound, cuts=(), held_as=jnp.bfloat16):
    loudness = steps_of(own_key, extent, cuts, -0.22, 0.18) if cuts else 1.0
    drawn = jax.random.normal(own_key, extent, jnp.float32) * scale * loudness
    return jnp.minimum(jnp.maximum(drawn, -bound), bound).astype(held_as)


def setup_inputs(seed: int = 0) -> dict:
    seeds = jax.random.split(jax.random.key(seed), 5)
    return {
        "image_features": gaussian(seeds[0], (ROWS, D), 0.03, 0.1796875, ((0, 256),)),
        "text_features": gaussian(seeds[1], (ROWS, D), 0.03, 0.1796875, ((0, 256),)),
        "image_head": gaussian(seeds[2], (D, D), D ** -0.5, 0.1875),
        "text_head": gaussian(seeds[3], (D, D), D ** -0.5, 0.1875),
    }


SCORE_SCALE = 10.0
SCORE_BIAS = -2.5
EPSILON = 1e-06

def normalize(features, weight_matrix):
    projected = jnp.dot(features, weight_matrix, preferred_element_type=jnp.float32)
    factor = lax.rsqrt(lax.optimization_barrier(jnp.sum(projected * projected, axis=-1, keepdims=True)) + EPSILON)
    return (projected * factor, factor)

def pair_weights(image_vectors, text_vectors, image_offset, text_offset):
    pair_scores = SCORE_SCALE * lax.dot_general(image_vectors, text_vectors, (((1,), (1,)), ((), ())), preferred_element_type=jnp.float32) + SCORE_BIAS
    row_ids = image_offset + lax.broadcasted_iota(jnp.int32, pair_scores.shape, 0)
    col_ids = text_offset + lax.broadcasted_iota(jnp.int32, pair_scores.shape, 1)
    match_targets = jnp.where(row_ids == col_ids, 1.0, -1.0).astype(jnp.float32)
    return (SCORE_SCALE * -match_targets * jax.nn.sigmoid(-match_targets * pair_scores)).astype(jnp.bfloat16)

def norm_back(unit, factor, gradient):
    return (factor * (gradient - unit * lax.optimization_barrier(jnp.sum(unit * gradient, axis=-1, keepdims=True)))).astype(jnp.bfloat16)

def block_head_sum(features, back):
    feature_count = features.shape[1]

    def one_block(running, pair):
        rows, grads = pair
        term = jnp.einsum('bi,bj->ij', rows.astype(jnp.float32), grads.astype(jnp.float32))
        return (running + term.astype(jnp.bfloat16).astype(jnp.float32), None)
    stacked = (features.reshape(-1, B, feature_count), back.reshape(-1, B, feature_count))
    total, unused = lax.scan(one_block, jnp.zeros((feature_count, feature_count), jnp.float32), stacked)
    return total

def reference(image_features, text_features, image_head, text_head):
    feature_count = image_features.shape[1]
    image_groups = image_features.reshape(N_CUTS, B * N_LOOP, feature_count)
    text_groups = text_features.reshape(N_CUTS, B * N_LOOP, feature_count)

    def one_group(running, blocks):
        image_block, text_block = blocks
        image_unit, image_factor = normalize(image_block, image_head)
        text_unit, text_factor = normalize(text_block, text_head)
        image_vectors = image_unit.astype(jnp.bfloat16)
        text_vectors = text_unit.astype(jnp.bfloat16)
        weights = pair_weights(image_vectors, text_vectors, 0, 0)
        image_pull = jnp.dot(weights, text_vectors, preferred_element_type=jnp.float32)
        text_attraction = lax.dot_general(weights, image_vectors, (((0,), (0,)), ((), ())), preferred_element_type=jnp.float32)
        image_back = norm_back(image_unit, image_factor, image_pull)
        text_back = norm_back(text_unit, text_factor, text_attraction)
        image_out = lax.dot_general(image_back, image_head, (((1,), (1,)), ((), ())), preferred_element_type=jnp.float32)
        text_out = lax.dot_general(text_back, text_head, (((1,), (1,)), ((), ())), preferred_element_type=jnp.float32)
        image_wgrad = block_head_sum(image_block, image_back)
        text_wgrad = block_head_sum(text_block, text_back)
        return ((running[0] + image_wgrad, running[1] + text_wgrad), (image_out, text_out))
    zeros_head = jnp.zeros((feature_count, feature_count), jnp.float32)
    heads, outs = lax.scan(one_group, (zeros_head, zeros_head), (image_groups, text_groups))
    image_grad = outs[0].reshape(-1, feature_count)
    text_grad = outs[1].reshape(-1, feature_count)
    return (image_grad, text_grad, heads[0], heads[1])
```

```python
import jax
import jax.numpy as jnp
from jax import lax
from jax.experimental import pallas as pl
from jax.experimental.pallas import tpu as pltpu
from jax.sharding import PartitionSpec as P

SCORE_SCALE = 10.0
SCORE_BIAS = -2.5
EPSILON = 1e-06

D = 1152
B = 256
HB = 128
NZ, NY, NX = 8, 4, 4
BLK = 8
BR = D // BLK
RT, CT = BR // 16, D // 128
NT = RT * CT
ZT = 11
TP = ZT * NZ
F32, BF16 = jnp.float32, jnp.bfloat16
MESH = pl.DeviceIdType.MESH


def kernel(
    fi_hbm, ft_hbm, hi_hbm, ht_hbm,
    gi_out, gt_out, wi_out, wt_out,
    fi, ft, hi, ht, x32, xb, sx, y32, yb, sy, w, wt, fit, ftt, g32, dpp, dqp,
    gsend, rx_opp, rx_l, rx_r, gysend, gyrecv, ysend, yrecv,
    tt, trecv, zh, zr, zs, pr, psum, zg, fin, finr,
    s_loc, s_fi, r_fi, s_ft, r_ft, s_yb, r_yb, s_gx, r_gx, s_gy, r_gy, s_y, r_y,
    s_t, r_t, s_z, r_z, s_p, r_p, s_g, r_g, s_f, r_f,
):
    cuts, loop = lax.axis_index("cuts"), lax.axis_index("loop")
    z, yh = cuts // 2, cuts % 2
    yl, x, core = loop // 8, (loop // 2) % 4, loop % 2
    me_plane = (yh * 2 + yl) * NX + x

    def dev(z_, yh_, yl_, x_, c_):
        return (z_ * 2 + yh_, (yl_ * NX + x_) * 2 + c_)

    right = dev(z, yh, yl, (x + 1) % NX, core)
    left = dev(z, yh, yl, (x + 3) % NX, core)
    mate = dev(z, yh, 1 - yl, x, core)
    sib = dev(z, yh, yl, x, 1 - core)
    zpeer = [dev((z + r) % NZ, yh, yl, x, core) for r in range(NZ)]
    up, down = zpeer[1], zpeer[7]

    def plane(r):
        q = (me_plane + r) % 16
        return dev(z, q // 8, (q // 4) % 2, q % 4, core), q % 8

    def local(src, dst, k):
        c = pltpu.make_async_copy(src, dst, s_loc.at[k])
        c.start()
        return c

    l_ft = local(ft_hbm, ft.at[0], 0)
    l_ht = local(ht_hbm, ht, 1)
    l_fi = local(fi_hbm, fi.at[0], 2)
    l_hi = local(hi_hbm, hi, 3)

    barrier = pltpu.get_barrier_semaphore()
    peers = [sib] + zpeer[1:] + [plane(r)[0] for r in range(1, 16)]
    for p in peers:
        pl.semaphore_signal(barrier, inc=1, device_id=p, device_id_type=MESH)
    pl.semaphore_wait(barrier, len(peers))

    def remote(src, dst, ss, rs, to):
        return pltpu.make_async_remote_copy(
            src_ref=src, dst_ref=dst, send_sem=ss, recv_sem=rs, device_id=to, device_id_type=MESH
        )

    A, Bh = pl.ds(0, HB), pl.ds(HB, HB)
    c_ra = remote(fi_hbm.at[A], fi.at[1, A], s_fi.at[0], r_fi.at[0], right)
    c_rb = remote(fi_hbm.at[Bh], fi.at[1, Bh], s_fi.at[1], r_fi.at[1], right)
    c_lb = remote(fi_hbm.at[Bh], fi.at[2, Bh], s_fi.at[2], r_fi.at[2], left)
    c_la = remote(fi_hbm.at[A], fi.at[2, A], s_fi.at[3], r_fi.at[3], left)
    c_ft = remote(ft_hbm, ft.at[1], s_ft.at[0], r_ft.at[0], mate)
    c_ra.start()
    c_lb.start()
    c_ft.start()
    c_rb.start()
    c_la.start()
    c_oa = remote(fi.at[1, A], fi.at[3, A], s_fi.at[4], r_fi.at[4], right)
    c_ob = remote(fi.at[2, Bh], fi.at[3, Bh], s_fi.at[5], r_fi.at[5], left)

    def normalize(f_ref, k, h_ref, v32, vb, s_ref):
        p = jnp.dot(f_ref[k], h_ref[...], preferred_element_type=F32)
        s = lax.rsqrt(jnp.sum(p * p, axis=-1, keepdims=True) + EPSILON)
        v = p * s
        v32[k] = v
        vb[k] = v.astype(BF16)
        s_ref[k] = s

    def flip(f_ref, k, t_ref):
        for j in range(CT):
            t_ref[pl.ds(j * 128, 128), pl.ds(k * B, B)] = f_ref[k, :, pl.ds(j * 128, 128)].T

    def weigh(i, j, own):
        sc = (
            SCORE_SCALE
            * lax.dot_general(xb[i], yb[j], (((1,), (1,)), ((), ())), preferred_element_type=F32)
            + SCORE_BIAS
        )
        half = (SCORE_SCALE * 0.5) * jnp.tanh(0.5 * sc)
        val = half + SCORE_SCALE * 0.5
        if own:
            same = lax.broadcasted_iota(jnp.int32, (B, B), 0) == lax.broadcasted_iota(
                jnp.int32, (B, B), 1
            )
            val = jnp.where(same, half - SCORE_SCALE * 0.5, val)
        w[i, :, pl.ds(j * B, B)] = val.astype(BF16)
        wt[j, :, pl.ds(i * B, B)] = val.T.astype(BF16)

    def pull(i):
        acc = jnp.dot(w[i, :, pl.ds(0, B)], yb[0], preferred_element_type=F32)
        for j in range(1, 4):
            acc += jnp.dot(w[i, :, pl.ds(j * B, B)], yb[j], preferred_element_type=F32)
        return acc

    def back(u, s, g):
        return (s * (g - u * jnp.sum(u * g, axis=-1, keepdims=True))).astype(BF16)

    c_yb = [remote(yb.at[k], yb.at[2 + k], s_yb.at[k], r_yb.at[k], sib) for k in range(2)]

    l_ft.wait()
    l_ht.wait()
    normalize(ft, 0, ht, y32, yb, sy)
    c_yb[0].start()
    l_fi.wait()
    l_hi.wait()
    normalize(fi, 0, hi, x32, xb, sx)
    weigh(0, 0, True)
    c_ra.wait_recv()
    c_oa.start()
    c_lb.wait_recv()
    c_ob.start()
    flip(fi, 0, fit)
    flip(ft, 0, ftt)
    c_yb[0].wait_recv()
    weigh(0, 2, False)
    c_ft.wait_recv()
    normalize(ft, 1, ht, y32, yb, sy)
    c_yb[1].start()
    c_rb.wait_recv()
    c_la.wait_recv()

    def neighbour(i, _):
        normalize(fi, i, hi, x32, xb, sx)
        return 0

    lax.fori_loop(1, 3, neighbour, 0)
    flip(ft, 1, ftt)
    flip(fi, 1, fit)
    flip(fi, 2, fit)
    weigh(0, 1, False)
    c_yb[1].wait_recv()
    weigh(0, 3, False)

    def tiles(k, _):
        weigh(1 + k // 4, k % 4, False)
        return 0

    lax.fori_loop(0, 8, tiles, 0)

    def image_pull(i, keep):
        g = pull(i)
        if keep is not None:
            keep[...] = g
        gsend[i] = g.astype(BF16)
        dpp[pl.ds(pl.multiple_of(i * B, B), B)] = back(x32[i], sx[i], g)

    def pull_neighbour(i, _):
        image_pull(i, g32.at[i - 1])
        return 0

    lax.fori_loop(1, 3, pull_neighbour, 0)
    c_nb = remote(gsend.at[2, Bh], rx_l.at[Bh], s_gx.at[0], r_gx.at[0], right)
    c_na = remote(gsend.at[1, A], rx_r.at[A], s_gx.at[1], r_gx.at[1], left)
    c_nb.start()
    c_na.start()
    image_pull(0, gi_out)

    c_oa.wait_recv()
    c_ob.wait_recv()
    normalize(fi, 3, hi, x32, xb, sx)

    def tiles_opp(k, _):
        weigh(3, k, False)
        return 0

    lax.fori_loop(0, 4, tiles_opp, 0)
    image_pull(3, None)
    c_pa = remote(gsend.at[3, A], rx_opp.at[A], s_gx.at[2], r_gx.at[2], right)
    c_pb = remote(gsend.at[3, Bh], rx_opp.at[Bh], s_gx.at[3], r_gx.at[3], left)
    c_pa.start()
    c_pb.start()
    flip(fi, 3, fit)

    def text_pull(j):
        acc = jnp.dot(wt[j, :, pl.ds(0, B)], xb[0], preferred_element_type=F32)
        for i in range(1, 4):
            acc += jnp.dot(wt[j, :, pl.ds(i * B, B)], xb[i], preferred_element_type=F32)
        return acc

    def for_sib(k, _):
        gysend[k] = text_pull(2 + k).astype(BF16)
        return 0

    lax.fori_loop(0, 2, for_sib, 0)
    c_gy = remote(gysend, gyrecv, s_gy, r_gy, sib)
    c_gy.start()

    g_mate = text_pull(1)
    gt_out[...] = text_pull(0)
    c_gy.wait_recv()
    g_mate += gyrecv[1].astype(F32)
    ysend[...] = g_mate.astype(BF16)
    c_y = remote(ysend, yrecv, s_y, r_y, mate)
    c_y.start()
    dqp[pl.ds(B, B)] = back(y32[1], sy[1], g_mate)
    g_own = gt_out[...] + gyrecv[0].astype(F32)
    gt_out[...] = g_own
    dqp[pl.ds(0, B)] = back(y32[0], sy[0], g_own)

    def head(f_t, d_ref, depth, slot):
        def row_block(b, _):
            o = jnp.dot(
                f_t[pl.ds(pl.multiple_of(b * BR, 16), BR), :], d_ref[...], preferred_element_type=F32
            ).astype(BF16)
            for r in range(RT):
                for c in range(CT):
                    tt[slot, b, c * RT + r] = o[r * 16 : r * 16 + 16, c * 128 : c * 128 + 128]
            return 0

        lax.fori_loop(0, BLK, row_block, 0)

    zero = jnp.zeros((BLK, TP - NT, 16, 128), BF16)
    tt[0, :, pl.ds(NT, TP - NT)] = zero
    tt[1, :, pl.ds(NT, TP - NT)] = zero
    c_t = remote(tt.at[1], trecv, s_t, r_t, sib)
    head(ftt, dqp, 2 * B, 1 - core)

    @pl.when(core == 0)
    def _():
        c_t.start()

    head(fit, dpp, 4 * B, core)

    @pl.when(core == 1)
    def _():
        c_t.start()

    c_pa.wait_recv()
    gsend[2, A] = (g32[1, A] + rx_opp[A].astype(F32)).astype(BF16)
    c_qa = remote(gsend.at[2, A], rx_l.at[A], s_gx.at[4], r_gx.at[4], right)
    c_qa.start()
    c_pb.wait_recv()
    gsend[1, Bh] = (g32[0, Bh] + rx_opp[Bh].astype(F32)).astype(BF16)
    c_qb = remote(gsend.at[1, Bh], rx_r.at[Bh], s_gx.at[5], r_gx.at[5], left)
    c_qb.start()

    c_t.wait_recv()

    def merge_t(b, _):
        tt[0, b] = (tt[0, b].astype(F32) + trecv[b].astype(F32)).astype(BF16)
        return 0

    lax.fori_loop(0, BLK, merge_t, 0)

    def piece(r):
        return pl.ds(ZT * ((z + r) % NZ), ZT)

    ZA = 6
    first_up = pl.ds(ZT * ((z + 4) % NZ), ZA)
    first_dn = pl.ds(ZT * ((z + 4) % NZ) + ZA, ZT - ZA)
    c_zu = remote(tt.at[0, :, first_up], zh.at[:, pl.ds(0, ZA)], s_z.at[0], r_z.at[0], up)
    c_zd = remote(tt.at[0, :, first_dn], zh.at[:, pl.ds(ZA, ZT - ZA)], s_z.at[1], r_z.at[1], down)
    c_zu.start()
    c_zd.start()
    sent = [c_zu, c_zd]
    for step in range(3):
        r = 3 - step
        c_zu.wait_recv()
        if step == 0:

            def add_up(b, _):
                zs[0, 0, b] = tt[0, b, piece(3)]
                zs[0, 0, b, pl.ds(0, ZA)] = (
                    tt[0, b, pl.ds(ZT * ((z + 3) % NZ), ZA)].astype(F32)
                    + zh[b, pl.ds(0, ZA)].astype(F32)
                ).astype(BF16)
                return 0

            def add_dn(b, _):
                zs[1, 0, b] = tt[0, b, piece(5)]
                zs[1, 0, b, pl.ds(ZA, ZT - ZA)] = (
                    tt[0, b, pl.ds(ZT * ((z + 5) % NZ) + ZA, ZT - ZA)].astype(F32)
                    + zh[b, pl.ds(ZA, ZT - ZA)].astype(F32)
                ).astype(BF16)
                return 0
        else:

            def add_up(b, _, step=step, r=r):
                zs[0, step, b] = (
                    tt[0, b, piece(r)].astype(F32) + zr[0, step - 1, b].astype(F32)
                ).astype(BF16)
                return 0

            def add_dn(b, _, step=step, r=r):
                zs[1, step, b] = (
                    tt[0, b, piece(8 - r)].astype(F32) + zr[1, step - 1, b].astype(F32)
                ).astype(BF16)
                return 0

        lax.fori_loop(0, BLK, add_up, 0)
        c_zu = remote(zs.at[0, step], zr.at[0, step], s_z.at[2 + 2 * step], r_z.at[2 + 2 * step], up)
        c_zu.start()
        c_zd.wait_recv()
        lax.fori_loop(0, BLK, add_dn, 0)
        c_zd = remote(
            zs.at[1, step], zr.at[1, step], s_z.at[3 + 2 * step], r_z.at[3 + 2 * step], down
        )
        c_zd.start()
        sent += [c_zu, c_zd]
        if step == 0:
            c_nb.wait_recv()
            c_na.wait_recv()
            c_qa.wait_recv()
            c_qb.wait_recv()
            dpf = back(x32[0], sx[0], gi_out[...] + rx_l[...].astype(F32) + rx_r[...].astype(F32))
            gi_out[...] = lax.dot_general(
                dpf, hi[...], (((1,), (1,)), ((), ())), preferred_element_type=F32
            )
        if step == 1:
            c_y.wait_recv()
            dqf = back(y32[0], sy[0], gt_out[...] + yrecv[...].astype(F32))
            gt_out[...] = lax.dot_general(
                dqf, ht[...], (((1,), (1,)), ((), ())), preferred_element_type=F32
            )
    c_zu.wait_recv()
    c_zd.wait_recv()

    def add_own(b, _):
        psum[b] = (
            tt[0, b, piece(0)].astype(F32) + zr[0, 2, b].astype(F32) + zr[1, 2, b].astype(F32)
        ).astype(BF16)
        return 0

    lax.fori_loop(0, BLK, add_own, 0)

    c_p = []
    for r in range(1, 16):
        to, blk = plane(r)
        c_p.append(remote(psum.at[blk], pr.at[r], s_p.at[r], r_p.at[r], to))
        c_p[-1].start()
    pr[0] = psum[me_plane % 8]
    for c in c_p:
        c.wait_recv()
    total = pr[me_plane].astype(F32)
    for q in range(1, 16):
        total += pr[(me_plane + 16 - q) % 16].astype(F32)
    zg[0] = total.astype(BF16)

    c_g = []
    for r in range(1, NZ):
        c_g.append(remote(zg.at[0], zg.at[r], s_g.at[r], r_g.at[r], zpeer[r]))
        c_g[-1].start()
    fin[pl.ds(ZT * z, ZT)] = zg[0]
    for r in range(1, NZ):
        c_g[r - 1].wait_recv()
        fin[pl.ds(ZT * ((z + 8 - r) % NZ), ZT)] = zg[r]
    c_f = remote(fin, finr, s_f, r_f, sib)
    c_f.start()
    c_f.wait_recv()

    def emit(ref, out, first):
        for c in range(CT):
            col = ref[pl.ds(c * RT, RT)].astype(F32).reshape(BR, 128)
            out[:, pl.ds(c * 128, 128)] = col[first : first + BR // 2]

    @pl.when(core == 0)
    def _():
        emit(fin, wi_out, 0)
        emit(finr, wt_out, 0)

    @pl.when(core == 1)
    def _():
        emit(finr, wi_out, BR // 2)
        emit(fin, wt_out, BR // 2)

    for c in (
        [c_ra, c_rb, c_lb, c_la, c_ft, c_oa, c_ob, c_nb, c_na, c_pa, c_pb, c_qa, c_qb, c_gy, c_y]
        + c_yb + [c_t, c_f] + sent + c_p + c_g
    ):
        c.wait_send()


def per_device(image_features, text_features, image_head, text_head):
    vm, dma = pltpu.VMEM, pltpu.SemaphoreType.DMA
    outs = (
        jax.ShapeDtypeStruct((B, D), F32),
        jax.ShapeDtypeStruct((B, D), F32),
        jax.ShapeDtypeStruct((BR // 2, D), F32),
        jax.ShapeDtypeStruct((BR // 2, D), F32),
    )
    return pl.pallas_call(
        kernel,
        out_shape=outs,
        in_specs=[pl.BlockSpec(memory_space=pl.ANY)] * 4,
        out_specs=[pl.BlockSpec(memory_space=pltpu.VMEM)] * 4,
        scratch_shapes=[
            vm((4, B, D), BF16), vm((2, B, D), BF16), vm((D, D), BF16), vm((D, D), BF16),
            vm((4, B, D), F32), vm((4, B, D), BF16), vm((4, B, 1), F32),
            vm((2, B, D), F32), vm((4, B, D), BF16), vm((2, B, 1), F32),
            vm((4, B, 4 * B), BF16), vm((4, B, 4 * B), BF16),
            vm((D, 4 * B), BF16), vm((D, 2 * B), BF16),
            vm((2, B, D), F32), vm((4 * B, D), BF16), vm((2 * B, D), BF16),
            vm((4, B, D), BF16), vm((B, D), BF16),
            vm((B, D), BF16), vm((B, D), BF16),
            vm((2, B, D), BF16), vm((2, B, D), BF16),
            vm((B, D), BF16), vm((B, D), BF16),
            vm((2, BLK, TP, 16, 128), BF16), vm((BLK, TP, 16, 128), BF16),
            vm((BLK, ZT, 16, 128), BF16), vm((2, 3, BLK, ZT, 16, 128), BF16),
            vm((2, 3, BLK, ZT, 16, 128), BF16), vm((16, ZT, 16, 128), BF16),
            vm((BLK, ZT, 16, 128), BF16), vm((NZ, ZT, 16, 128), BF16),
            vm((TP, 16, 128), BF16), vm((TP, 16, 128), BF16),
            dma((4,)), dma((6,)), dma((6,)), dma((1,)), dma((1,)), dma((2,)), dma((2,)),
            dma((6,)), dma((6,)), dma(()), dma(()), dma(()), dma(()),
            dma(()), dma(()), dma((8,)), dma((8,)), dma((16,)), dma((16,)),
            dma((8,)), dma((8,)), dma(()), dma(()),
        ],
        compiler_params=pltpu.CompilerParams(
            collective_id=0, has_side_effects=True, vmem_limit_bytes=63 << 20
        ),
        name="siglip_back",
    )(image_features, text_features, image_head, text_head)


def solution(mesh):
    placed = (P(("cuts", "loop"), None), P(("cuts", "loop"), None), P(), P())
    return jax.shard_map(
        per_device,
        mesh=mesh,
        in_specs=placed,
        out_specs=(
            P(("cuts", "loop"), None),
            P(("cuts", "loop"), None),
            P("loop", None),
            P("loop", None),
        ),
        check_vma=False,
    )
```

```python
import jax
import jax.numpy as jnp
from jax import lax
from jax.experimental import pallas as pl
from jax.experimental.pallas import tpu as pltpu
from jax.sharding import PartitionSpec as P

SCORE_SCALE = 10.0
SCORE_BIAS = -2.5
EPSILON = 1e-06

D = 1152
B = 256
HB = 128
NZ, NY, NX = 8, 4, 4
BLK = 8
BR = D // BLK
RT, CT = BR // 16, D // 128
NT = RT * CT
ZH = 3
ZT = 2 * ZH
ZN = ZT * NZ
YT = (NT - ZN + 1) // 2
TP = ZN + 2 * YT
YP = 3
YW = YP * NZ
FIN = ZN + 2 * YW
F32, BF16 = jnp.float32, jnp.bfloat16
MESH = pl.DeviceIdType.MESH
NT_DIMS = (((1,), (1,)), ((), ()))
TN_DIMS = (((0,), (0,)), ((), ()))


def kernel(
    fi_hbm, ft_hbm, hi_hbm, ht_hbm,
    gi_hbm, gt_hbm, wi_hbm, wt_hbm,
    fi, ft, hi, ht, x32, xb, sx, y32, yb, sy, w, wt, gi, gt, g2, dpp, dqp,
    gsend, rx_opp, rx_l, rx_r, gysend, gyrecv, ysend, yrecv,
    tt, trecv, zr, zs, yr, ys, ysum, xr, xsum, qr, qg, psum, pr, zg, fin, finr, wi, wo,
    s_loc, s_fi, r_fi, s_ft, r_ft, s_yb, r_yb, s_gx, r_gx, s_gy, r_gy, s_y, r_y,
    s_t, r_t, s_z, r_z, s_yr, r_yr, s_x, r_x, s_q, r_q, s_k, r_k, s_p, r_p, s_g, r_g, s_f, r_f, s_out,
):
    cuts, loop = lax.axis_index("cuts"), lax.axis_index("loop")
    z, yh = cuts // 2, cuts % 2
    yl, x, core = loop // 8, (loop // 2) % 4, loop % 2
    yp = yh * 2 + yl
    me_plane = yp * NX + x

    def dev(z_, yp_, x_, c_):
        return (z_ * 2 + yp_ // 2, ((yp_ % 2) * NX + x_) * 2 + c_)

    xpeer = [dev(z, yp, (x + r) % NX, core) for r in range(NX)]
    ypeer = [dev(z, (yp + r) % NY, x, core) for r in range(NY)]
    zpeer = [dev((z + r) % NZ, yp, x, core) for r in range(NZ)]
    right, left = xpeer[1], xpeer[3]
    mate = dev(z, yh * 2 + 1 - yl, x, core)
    sib = dev(z, yp, x, 1 - core)

    def plane(r):
        q = (me_plane + r) % 16
        return dev(z, q // 4, q % 4, core), q % 8

    def local(src, dst, k):
        c = pltpu.make_async_copy(src, dst, s_loc.at[k])
        c.start()
        return c

    barrier = pltpu.get_barrier_semaphore()
    peers = [sib, right, left, ypeer[1], ypeer[3], zpeer[1], zpeer[7]]
    for p in peers:
        pl.semaphore_signal(barrier, inc=1, device_id=p, device_id_type=MESH)
    l_ft = local(ft_hbm, ft.at[0], 0)
    l_ht = local(ht_hbm, ht, 1)
    l_fi = local(fi_hbm, fi.at[0], 2)
    l_hi = local(hi_hbm, hi, 3)
    pl.semaphore_wait(barrier, len(peers))

    def remote(src, dst, ss, rs, to):
        return pltpu.make_async_remote_copy(
            src_ref=src, dst_ref=dst, send_sem=ss, recv_sem=rs, device_id=to, device_id_type=MESH
        )

    A, Bh = pl.ds(0, HB), pl.ds(HB, HB)
    c_ra = remote(fi_hbm.at[A], fi.at[1, A], s_fi.at[0], r_fi.at[0], right)
    c_lb = remote(fi_hbm.at[Bh], fi.at[1, Bh], s_fi.at[1], r_fi.at[1], left)
    c_rb = remote(fi_hbm.at[Bh], fi.at[2, Bh], s_fi.at[2], r_fi.at[2], right)
    c_la = remote(fi_hbm.at[A], fi.at[2, A], s_fi.at[3], r_fi.at[3], left)
    c_ft = remote(ft_hbm, ft.at[1], s_ft, r_ft, mate)
    c_ra.start()
    c_lb.start()
    c_ft.start()
    c_rb.start()
    c_la.start()
    c_oa = remote(fi.at[1, A], fi.at[3, A], s_fi.at[4], r_fi.at[4], right)
    c_ob = remote(fi.at[1, Bh], fi.at[3, Bh], s_fi.at[5], r_fi.at[5], left)

    def normalize(f, h_ref, v32, vb, s_ref):
        p = jnp.dot(f, h_ref[...], preferred_element_type=F32)
        s = lax.rsqrt(jnp.sum(p * p, axis=-1, keepdims=True) + EPSILON)
        v = p * s
        v32[...] = v
        vb[...] = v.astype(BF16)
        s_ref[...] = s

    place = (0, 2, 1, 3)

    def weigh(i0, m, j0, n):
        dots = lax.dot_general(
            xb[pl.ds(i0, m)].reshape(m * B, D), yb[pl.ds(j0, n)].reshape(n * B, D), NT_DIMS,
            preferred_element_type=F32,
        )
        for i in range(m):
            for j in range(n):
                sc = SCORE_SCALE * dots[i * B : i * B + B, j * B : j * B + B] + SCORE_BIAS
                half = (SCORE_SCALE * 0.5) * jnp.tanh(0.5 * sc)
                val = half + SCORE_SCALE * 0.5
                if i0 + i == 0 and j0 + j == 0:
                    same = lax.broadcasted_iota(jnp.int32, (B, B), 0) == lax.broadcasted_iota(
                        jnp.int32, (B, B), 1
                    )
                    val = jnp.where(same, half - SCORE_SCALE * 0.5, val)
                w[i0 + i, :, pl.ds((j0 + j) * B, B)] = val.astype(BF16)
                wt[place[j0 + j], :, pl.ds((i0 + i) * B, B)] = val.T.astype(BF16)

    def pull(i):
        return jnp.dot(w[i], yb[...].reshape(4 * B, D), preferred_element_type=F32)

    def back(u, s, g):
        return (s * (g - u * jnp.sum(u * g, axis=-1, keepdims=True))).astype(BF16)

    c_yb = [remote(yb.at[2 * k], yb.at[2 * k + 1], s_yb.at[k], r_yb.at[k], sib) for k in range(2)]

    l_ft.wait()
    l_ht.wait()
    normalize(ft[0], ht, y32.at[0], yb.at[0], sy.at[0])
    c_yb[0].start()
    l_fi.wait()
    l_hi.wait()
    normalize(fi[0], hi, x32.at[0], xb.at[0], sx.at[0])
    c_yb[0].wait_recv()
    weigh(0, 1, 0, 2)
    c_ra.wait_recv()
    c_oa.start()
    c_lb.wait_recv()
    c_ob.start()
    normalize(fi[1], hi, x32.at[1], xb.at[1], sx.at[1])
    weigh(1, 1, 0, 2)
    c_ft.wait_recv()
    normalize(ft[1], ht, y32.at[1], yb.at[2], sy.at[1])
    c_yb[1].start()
    c_rb.wait_recv()
    c_la.wait_recv()
    normalize(fi[2], hi, x32.at[2], xb.at[2], sx.at[2])
    weigh(2, 1, 0, 2)
    weigh(0, 3, 2, 1)
    c_yb[1].wait_recv()
    weigh(0, 3, 3, 1)

    def image_pull(i, keep):
        g = pull(i)
        if keep is not None:
            keep[...] = g
        if i:
            gsend[i - 1] = g.astype(BF16)
        dpp[pl.ds(i * B, B)] = back(x32[i], sx[i], g)

    image_pull(1, None)
    c_nb = remote(gsend.at[0, Bh], rx_l.at[Bh], s_gx.at[0], r_gx.at[0], right)
    c_na = remote(gsend.at[0, A], rx_r.at[A], s_gx.at[1], r_gx.at[1], left)
    c_nb.start()
    c_na.start()
    c_oa.wait_recv()
    c_ob.wait_recv()
    normalize(fi[3], hi, x32.at[3], xb.at[3], sx.at[3])
    weigh(3, 1, 0, 4)
    image_pull(3, None)
    c_pa = remote(gsend.at[2, A], rx_opp.at[A], s_gx.at[2], r_gx.at[2], right)
    c_pb = remote(gsend.at[2, Bh], rx_opp.at[Bh], s_gx.at[3], r_gx.at[3], left)
    c_pa.start()
    c_pb.start()

    def text_pull(j0):
        return jnp.dot(
            wt[pl.ds(j0, 2)].reshape(2 * B, 4 * B), xb[...].reshape(4 * B, D),
            preferred_element_type=F32,
        )

    gysend[...] = text_pull(2).astype(BF16)
    c_gy = remote(gysend, gyrecv, s_gy, r_gy, sib)
    c_gy.start()
    image_pull(0, gi)
    image_pull(2, g2)
    gt[...] = text_pull(0)

    thirds = ((0, 2), (2, 3), (5, 3))

    def t_copy(slot, k):
        at = pl.ds(*thirds[k])
        return remote(tt.at[slot, at], trecv.at[at], s_t.at[k], r_t.at[k], sib)

    c_t = [t_copy(0, k) for k in range(3)]
    CH = D // 3

    def head(f_ref, d_ref, slot, sender):
        f = f_ref[...].reshape(-1, D)
        for k in range(3):
            o = lax.dot_general(
                f[:, k * CH : (k + 1) * CH], d_ref[...], TN_DIMS, preferred_element_type=F32
            ).astype(BF16)
            a = 0
            while a < CH // 16:
                b, r = divmod(k * (CH // 16) + a, RT)
                n = min(RT - r, CH // 16 - a)
                for c in range(CT):
                    tt[slot, b, pl.ds(c * RT + r, n)] = o[
                        a * 16 : (a + n) * 16, c * 128 : c * 128 + 128
                    ].reshape(n, 16, 128)
                a += n

            @pl.when(core == sender)
            def _(k=k):
                t_copy(slot, k).start()

    if TP > NT:
        zero = jnp.zeros((BLK, TP - NT, 16, 128), BF16)
        tt[0, :, pl.ds(NT, TP - NT)] = zero
        tt[1, :, pl.ds(NT, TP - NT)] = zero
    head(fi, dpp, 0, 1)
    c_gy.wait_recv()
    g = gt[...] + gyrecv[...].reshape(2 * B, D).astype(F32)
    gt[...] = g
    ysend[...] = g[B:].astype(BF16)
    dqp[...] = back(y32[...].reshape(2 * B, D), sy[...].reshape(2 * B, 1), g)
    head(ft, dqp, 1, 0)

    c_pa.wait_recv()
    c_pb.wait_recv()
    gsend[1] = (g2[...] + rx_opp[...].astype(F32)).astype(BF16)
    c_qa = remote(gsend.at[1, A], rx_l.at[A], s_gx.at[4], r_gx.at[4], right)
    c_qb = remote(gsend.at[1, Bh], rx_r.at[Bh], s_gx.at[5], r_gx.at[5], left)

    for k, (b0, nb) in enumerate(thirds):
        c_t[k].wait_recv()
        for kept in range(2):

            def merge_t(b, _, kept=kept):
                trecv[b] = (tt[kept, b].astype(F32) + trecv[b].astype(F32)).astype(BF16)
                return 0

            @pl.when(core == kept)
            def _(b0=b0, nb=nb, merge_t=merge_t):
                lax.fori_loop(b0, b0 + nb, merge_t, 0)

    def zpiece(d, half, r):
        return pl.ds(ZT * ((z + (r if d == 0 else NZ - r)) % NZ) + ZH * half, ZH)

    order = [[(d, 4)] + [m for r in (3, 2, 1) for m in ((1 - d, r), (d, r))] for d in range(2)]
    cz = [[None] * 7, [None] * 7]

    def z_send(d, k):
        half, r = order[d][k]
        if k < 2:
            src = trecv.at[:, zpiece(d, half, r)]
        else:
            cz[d][k - 2].wait_recv()

            def add(b, _):
                zs[d, k - 2, b] = (
                    trecv[b, zpiece(d, half, r)].astype(F32) + zr[d, k - 2, b].astype(F32)
                ).astype(BF16)
                return 0

            lax.fori_loop(0, BLK, add, 0)
            src = zs.at[d, k - 2]
        cz[d][k] = remote(src, zr.at[d, k], s_z.at[d, k], r_z.at[d, k], zpeer[1 if d == 0 else 7])
        cz[d][k].start()

    def ypiece(r, half):
        t = (yp + r) % NY
        return pl.ds(4 * (t % 2) + 2 * half, 2), pl.ds(ZN + YT * (t // 2), YT)

    cy = [[None] * 3, [None] * 3]

    def y_send(d, k):
        to = ypeer[1 if d == 0 else 3]
        half = d if k != 1 else 1 - d
        bs, ts = ypiece(2 if k == 0 else (1 if d == 0 else 3), half)
        src = trecv.at[bs, ts]
        if k == 2:
            cy[d][0].wait_recv()
            ys[d] = (trecv[bs, ts].astype(F32) + yr[d, 0].astype(F32)).astype(BF16)
            src = ys.at[d]
        cy[d][k] = remote(src, yr.at[d, k], s_yr.at[d, k], r_yr.at[d, k], to)
        cy[d][k].start()

    for k in range(2):
        for d in range(2):
            z_send(d, k)
            y_send(d, k)
    c_qa.start()
    c_qb.start()
    z_send(0, 2)
    z_send(1, 2)
    y_send(0, 2)
    y_send(1, 2)
    for k in (3, 4, 5):
        z_send(0, k)
        z_send(1, k)
    for half, parts in ((0, ((0, 2), (1, 1))), (1, ((0, 1), (1, 2)))):
        bs, ts = ypiece(0, half)
        v = trecv[bs, ts].astype(F32)
        for d, k in parts:
            cy[d][k].wait_recv()
            v += yr[d, k].astype(F32)
        ysum[pl.ds(2 * half, 2)] = v.astype(BF16)
    c_x = []
    for r in range(1, NX):
        c_x.append(remote(ysum.at[(x + r) % NX], xr.at[r], s_x.at[r], r_x.at[r], xpeer[r]))
        c_x[-1].start()
    c_y = remote(ysend, yrecv, s_y, r_y, mate)
    c_y.start()
    z_send(0, 6)
    z_send(1, 6)
    v = ysum[x].astype(F32)
    for r in range(1, NX):
        c_x[r - 1].wait_recv()
        v += xr[r].astype(F32)
    xsum[pl.ds(0, YT)] = v.astype(BF16)
    xsum[pl.ds(YT, YW - YT)] = jnp.zeros((YW - YT, 16, 128), BF16)
    c_q = []
    for r in range(1, NZ):
        c_q.append(
            remote(xsum.at[pl.ds(YP * ((z + r) % NZ), YP)], qr.at[r], s_q.at[r], r_q.at[r], zpeer[r])
        )
        c_q[-1].start()
    for half, parts in ((0, ((0, 6), (1, 5))), (1, ((0, 5), (1, 6)))):
        for d, k in parts:
            cz[d][k].wait_recv()

        def own(b, _, half=half, parts=parts):
            v = trecv[b, zpiece(0, half, 0)].astype(F32)
            for d, k in parts:
                v += zr[d, k, b].astype(F32)
            psum[b, pl.ds(ZH * half, ZH)] = v.astype(BF16)
            return 0

        lax.fori_loop(0, BLK, own, 0)
    c_p = []
    for r in range(1, 16):
        to, blk = plane(r)
        c_p.append(remote(psum.at[blk], pr.at[r], s_p.at[r], r_p.at[r], to))
        c_p[-1].start()
    pr[0] = psum[me_plane % 8]
    v = xsum[pl.ds(YP * z, YP)].astype(F32)
    for r in range(1, NZ):
        c_q[r - 1].wait_recv()
        v += qr[r].astype(F32)
    qg[0] = v.astype(BF16)
    c_k = []
    for r in range(1, 16):
        dz, dy = r % 8, r // 8
        to = dev((z + dz) % NZ, (yp + 2 * dy) % NY, x, core)
        c_k.append(remote(qg.at[0], qg.at[r], s_k.at[r], r_k.at[r], to))
        c_k[-1].start()
    for c in c_p:
        c.wait_recv()
    total = pr[me_plane].astype(F32)
    for q in range(1, 16):
        total += pr[(me_plane + 16 - q) % 16].astype(F32)
    zg[0] = total.astype(BF16)
    c_g = []
    for r in range(1, NZ):
        c_g.append(remote(zg.at[0], zg.at[r], s_g.at[r], r_g.at[r], zpeer[r]))
        c_g[-1].start()

    outs = []

    def put(src, dst):
        outs.append(pltpu.make_async_copy(src, dst, s_out.at[len(outs)]))
        outs[-1].start()

    for c in (c_nb, c_na, c_qa, c_qb):
        c.wait_recv()
    dpf = back(x32[0], sx[0], gi[...] + rx_l[...].astype(F32) + rx_r[...].astype(F32))
    gi[...] = lax.dot_general(dpf, hi[...], NT_DIMS, preferred_element_type=F32)
    put(gi, gi_hbm)
    c_y.wait_recv()
    dqf = back(y32[0], sy[0], gt[pl.ds(0, B)] + yrecv[...].astype(F32))
    gt[pl.ds(0, B)] = lax.dot_general(dqf, ht[...], NT_DIMS, preferred_element_type=F32)
    put(gt.at[pl.ds(0, B)], gt_hbm)

    fin[pl.ds(ZN + YW * yh + YP * z, YP)] = qg[0]
    for r in range(1, 16):
        dz, dy = r % 8, r // 8
        c_k[r - 1].wait_recv()
        fin[pl.ds(ZN + YW * ((yh + dy) % 2) + YP * ((z + NZ - dz) % NZ), YP)] = qg[r]
    rest, front = pl.ds(ZN, FIN - ZN), pl.ds(0, ZN)
    c_fr = remote(fin.at[rest], finr.at[rest], s_f.at[0], r_f.at[0], sib)
    c_fr.start()
    fin[pl.ds(ZT * z, ZT)] = zg[0]
    for r in range(1, NZ):
        c_g[r - 1].wait_recv()
        fin[pl.ds(ZT * ((z + NZ - r) % NZ), ZT)] = zg[r]
    c_ff = remote(fin.at[front], finr.at[front], s_f.at[1], r_f.at[1], sib)
    c_ff.start()

    def emit(ref, out, first):
        def place_of(t):
            return t if t < ZN else ZN + YW * ((t - ZN) // YT) + (t - ZN) % YT

        r0, r1 = first // 16, -(-(first + BR // 2) // 16)
        for c in range(CT):
            r = r0
            while r < r1:
                t, n = place_of(c * RT + r), 1
                while r + n < r1 and place_of(c * RT + r + n) == t + n:
                    n += 1
                lo, up_ = max(r * 16, first), min((r + n) * 16, first + BR // 2)
                rows = ref[pl.ds(t, n)].astype(F32).reshape(n * 16, 128)
                out[pl.ds(lo - first, up_ - lo), pl.ds(c * 128, 128)] = rows[
                    lo - r * 16 : up_ - r * 16
                ]
                r += n

    @pl.when(core == 0)
    def _():
        emit(fin, wi, 0)
        c_fr.wait_recv()
        c_ff.wait_recv()
        emit(finr, wo, 0)

    @pl.when(core == 1)
    def _():
        emit(fin, wo, BR // 2)
        c_fr.wait_recv()
        c_ff.wait_recv()
        emit(finr, wi, BR // 2)

    put(wi, wi_hbm)
    put(wo, wt_hbm)
    for c in (
        [c_ra, c_rb, c_lb, c_la, c_ft, c_oa, c_ob, c_nb, c_na, c_pa, c_pb, c_qa, c_qb, c_gy, c_y]
        + c_yb + c_t + cz[0] + cz[1] + cy[0] + cy[1] + c_x + c_q + c_p + c_k + c_g + [c_fr, c_ff]
    ):
        c.wait_send()
    for c in outs:
        c.wait()


def hand_on(*refs):
    ins, outs, bufs, sem_in, sem_out = refs[:4], refs[4:8], refs[8:12], refs[12], refs[13]
    parts = []
    for a, o, v in zip(ins, outs, bufs):
        n = 2 if a.shape[0] == B else 1
        rows = a.shape[0] // n
        for k in range(n):
            at = pl.ds(k * rows, rows)
            parts.append(
                (
                    pltpu.make_async_copy(a.at[at], v.at[at], sem_in.at[len(parts)]),
                    pltpu.make_async_copy(v.at[at], o.at[at], sem_out.at[len(parts)]),
                )
            )
    for c, _ in parts:
        c.start()
    for c, d in parts:
        c.wait()
        d.start()
    for _, d in parts:
        d.wait()


def per_device(image_features, text_features, image_head, text_head):
    vm, dma = pltpu.VMEM, pltpu.SemaphoreType.DMA
    outs = (
        jax.ShapeDtypeStruct((B, D), F32),
        jax.ShapeDtypeStruct((B, D), F32),
        jax.ShapeDtypeStruct((BR // 2, D), F32),
        jax.ShapeDtypeStruct((BR // 2, D), F32),
    )
    tile = (16, 128)
    got = pl.pallas_call(
        kernel,
        out_shape=outs,
        in_specs=[pl.BlockSpec(memory_space=pl.ANY)] * 4,
        out_specs=[pl.BlockSpec(memory_space=pl.ANY)] * 4,
        scratch_shapes=[
            vm((4, B, D), BF16), vm((2, B, D), BF16), vm((D, D), BF16), vm((D, D), BF16),
            vm((4, B, D), F32), vm((4, B, D), BF16), vm((4, B, 1), F32),
            vm((2, B, D), F32), vm((4, B, D), BF16), vm((2, B, 1), F32),
            vm((4, B, 4 * B), BF16), vm((4, B, 4 * B), BF16),
            vm((B, D), F32), vm((2 * B, D), F32), vm((B, D), F32),
            vm((4 * B, D), BF16), vm((2 * B, D), BF16),
            vm((3, B, D), BF16), vm((B, D), BF16), vm((B, D), BF16), vm((B, D), BF16),
            vm((2 * B, D), BF16), vm((2 * B, D), BF16),
            vm((B, D), BF16), vm((B, D), BF16),
            vm((2, BLK, TP) + tile, BF16), vm((BLK, TP) + tile, BF16),
            vm((2, 7, BLK, ZH) + tile, BF16), vm((2, 5, BLK, ZH) + tile, BF16),
            vm((2, 3, 2, YT) + tile, BF16), vm((2, 2, YT) + tile, BF16),
            vm((4, YT) + tile, BF16), vm((4, YT) + tile, BF16),
            vm((YW,) + tile, BF16), vm((NZ, YP) + tile, BF16), vm((16, YP) + tile, BF16),
            vm((BLK, ZT) + tile, BF16), vm((16, ZT) + tile, BF16), vm((NZ, ZT) + tile, BF16),
            vm((FIN,) + tile, BF16), vm((FIN,) + tile, BF16),
            vm((BR // 2, D), F32), vm((BR // 2, D), F32),
            dma((4,)), dma((6,)), dma((6,)), dma(()), dma(()), dma((2,)), dma((2,)),
            dma((6,)), dma((6,)), dma(()), dma(()), dma(()), dma(()),
            dma((3,)), dma((3,)), dma((2, 7)), dma((2, 7)), dma((2, 3)), dma((2, 3)),
            dma((4,)), dma((4,)), dma((8,)), dma((8,)), dma((16,)), dma((16,)), dma((16,)), dma((16,)),
            dma((8,)), dma((8,)), dma((2,)), dma((2,)), dma((4,)),
        ],
        compiler_params=pltpu.CompilerParams(
            collective_id=0, has_side_effects=True, vmem_limit_bytes=63 << 20
        ),
        name="siglip_back",
    )(image_features, text_features, image_head, text_head)
    return pl.pallas_call(
        hand_on,
        out_shape=outs,
        in_specs=[pl.BlockSpec(memory_space=pl.ANY)] * 4,
        out_specs=[pl.BlockSpec(memory_space=pl.ANY)] * 4,
        scratch_shapes=[vm(o.shape, F32) for o in outs] + [dma((6,)), dma((6,))],
        name="hand_on",
    )(*got)


def solution(mesh):
    placed = (P(("cuts", "loop"), None), P(("cuts", "loop"), None), P(), P())
    return jax.shard_map(
        per_device,
        mesh=mesh,
        in_specs=placed,
        out_specs=(
            P(("cuts", "loop"), None),
            P(("cuts", "loop"), None),
            P("loop", None),
            P("loop", None),
        ),
        check_vma=False,
    )
```

```python
import jax
import jax.numpy as jnp
from jax import lax
from jax.experimental import pallas as pl
from jax.experimental.pallas import tpu as pltpu
from jax.sharding import PartitionSpec as P

SCORE_SCALE = 10.0
SCORE_BIAS = -2.5
EPSILON = 1e-06

D = 1152
B = 256
HB = 128
NZ, NY, NX = 8, 4, 4
BLK = 8
BR = D // BLK
RT, CT = BR // 16, D // 128
NT = RT * CT
ZH = 3
ZT = 2 * ZH
ZN = ZT * NZ
YT = (NT - ZN + 1) // 2
TP = ZN + 2 * YT
YP = 3
YW = YP * NZ
FIN = ZN + 2 * YW
F32, BF16 = jnp.float32, jnp.bfloat16
MESH = pl.DeviceIdType.MESH
NT_DIMS = (((1,), (1,)), ((), ()))
TN_DIMS = (((0,), (0,)), ((), ()))


def kernel(
    fi_hbm, ft_hbm, hi_hbm, ht_hbm,
    gi_hbm, gt_hbm, wi_hbm, wt_hbm,
    fi, ft, hi, ht, x32, xb, sx, y32, yb, sy, w, wt, gi, gt, g2, dpp, dqp,
    gsend, rx_opp, rx_l, rx_r, gysend, gyrecv, ysend, yrecv,
    tt, trecv, zr, zs, yr, ys, ysum, xr, xsum, qr, qg, psum, pr, zg, fin, finr, wi, wo,
    s_loc, s_fi, r_fi, s_ft, r_ft, s_yb, r_yb, s_gx, r_gx, s_gy, r_gy, s_y, r_y,
    s_t, r_t, s_z, r_z, s_yr, r_yr, s_x, r_x, s_q, r_q, s_k, r_k, s_p, r_p, s_g, r_g, s_f, r_f, s_out,
):
    cuts, loop = lax.axis_index("cuts"), lax.axis_index("loop")
    z, yh = cuts // 2, cuts % 2
    yl, x, core = loop // 8, (loop // 2) % 4, loop % 2
    yp = yh * 2 + yl
    me_plane = yp * NX + x

    def dev(z_, yp_, x_, c_):
        return (z_ * 2 + yp_ // 2, ((yp_ % 2) * NX + x_) * 2 + c_)

    xpeer = [dev(z, yp, (x + r) % NX, core) for r in range(NX)]
    ypeer = [dev(z, (yp + r) % NY, x, core) for r in range(NY)]
    zpeer = [dev((z + r) % NZ, yp, x, core) for r in range(NZ)]
    right, left = xpeer[1], xpeer[3]
    mate = dev(z, yh * 2 + 1 - yl, x, core)
    sib = dev(z, yp, x, 1 - core)

    def plane(r):
        q = (me_plane + r) % 16
        return dev(z, q // 4, q % 4, core), q % 8

    def local(src, dst, k):
        c = pltpu.make_async_copy(src, dst, s_loc.at[k])
        c.start()
        return c

    barrier = pltpu.get_barrier_semaphore()
    peers = [sib, right, left, ypeer[1], ypeer[3], zpeer[1], zpeer[7]]
    for p in peers:
        pl.semaphore_signal(barrier, inc=1, device_id=p, device_id_type=MESH)
    l_ft = local(ft_hbm, ft.at[0], 0)
    l_ht = local(ht_hbm, ht, 1)
    l_fi = local(fi_hbm, fi.at[0], 2)
    l_hi = local(hi_hbm, hi, 3)
    pl.semaphore_wait(barrier, len(peers))

    def remote(src, dst, ss, rs, to):
        return pltpu.make_async_remote_copy(
            src_ref=src, dst_ref=dst, send_sem=ss, recv_sem=rs, device_id=to, device_id_type=MESH
        )

    A, Bh = pl.ds(0, HB), pl.ds(HB, HB)
    c_ra = remote(fi_hbm.at[A], fi.at[1, A], s_fi.at[0], r_fi.at[0], right)
    c_lb = remote(fi_hbm.at[Bh], fi.at[1, Bh], s_fi.at[1], r_fi.at[1], left)
    c_rb = remote(fi_hbm.at[Bh], fi.at[2, Bh], s_fi.at[2], r_fi.at[2], right)
    c_la = remote(fi_hbm.at[A], fi.at[2, A], s_fi.at[3], r_fi.at[3], left)
    c_ft = remote(ft_hbm, ft.at[1], s_ft, r_ft, mate)
    c_ra.start()
    c_lb.start()
    c_ft.start()
    c_rb.start()
    c_la.start()
    c_oa = remote(fi.at[1, A], fi.at[3, A], s_fi.at[4], r_fi.at[4], right)
    c_ob = remote(fi.at[1, Bh], fi.at[3, Bh], s_fi.at[5], r_fi.at[5], left)

    def normalize(f, h_ref, v32, vb, s_ref):
        p = jnp.dot(f, h_ref[...], preferred_element_type=F32)
        s = lax.rsqrt(jnp.sum(p * p, axis=-1, keepdims=True) + EPSILON)
        v = p * s
        v32[...] = v
        vb[...] = v.astype(BF16)
        s_ref[...] = s

    place = (0, 2, 1, 3)

    def weigh(i0, m, j0, n):
        dots = lax.dot_general(
            xb[pl.ds(i0, m)].reshape(m * B, D), yb[pl.ds(j0, n)].reshape(n * B, D), NT_DIMS,
            preferred_element_type=F32,
        )
        for i in range(m):
            for j in range(n):
                sc = SCORE_SCALE * dots[i * B : i * B + B, j * B : j * B + B] + SCORE_BIAS
                half = (SCORE_SCALE * 0.5) * jnp.tanh(0.5 * sc)
                val = half + SCORE_SCALE * 0.5
                if i0 + i == 0 and j0 + j == 0:
                    same = lax.broadcasted_iota(jnp.int32, (B, B), 0) == lax.broadcasted_iota(
                        jnp.int32, (B, B), 1
                    )
                    val = jnp.where(same, half - SCORE_SCALE * 0.5, val)
                w[i0 + i, :, pl.ds((j0 + j) * B, B)] = val.astype(BF16)
                wt[place[j0 + j], :, pl.ds((i0 + i) * B, B)] = val.T.astype(BF16)

    def pull(i):
        return jnp.dot(w[i], yb[...].reshape(4 * B, D), preferred_element_type=F32)

    def back(u, s, g):
        return (s * (g - u * jnp.sum(u * g, axis=-1, keepdims=True))).astype(BF16)

    c_yb = [remote(yb.at[2 * k], yb.at[2 * k + 1], s_yb.at[k], r_yb.at[k], sib) for k in range(2)]

    l_ft.wait()
    l_ht.wait()
    normalize(ft[0], ht, y32.at[0], yb.at[0], sy.at[0])
    c_yb[0].start()
    l_fi.wait()
    l_hi.wait()
    normalize(fi[0], hi, x32.at[0], xb.at[0], sx.at[0])
    c_yb[0].wait_recv()
    weigh(0, 1, 0, 2)
    c_ra.wait_recv()
    c_oa.start()
    c_lb.wait_recv()
    c_ob.start()
    normalize(fi[1], hi, x32.at[1], xb.at[1], sx.at[1])
    weigh(1, 1, 0, 2)
    c_ft.wait_recv()
    normalize(ft[1], ht, y32.at[1], yb.at[2], sy.at[1])
    c_yb[1].start()
    c_rb.wait_recv()
    c_la.wait_recv()
    normalize(fi[2], hi, x32.at[2], xb.at[2], sx.at[2])
    weigh(2, 1, 0, 2)
    weigh(0, 3, 2, 1)
    c_yb[1].wait_recv()
    weigh(0, 3, 3, 1)

    def image_pull(i, keep):
        g = pull(i)
        if keep is not None:
            keep[...] = g
        if i:
            gsend[i - 1] = g.astype(BF16)
        dpp[pl.ds(i * B, B)] = back(x32[i], sx[i], g)

    image_pull(1, None)
    c_nb = remote(gsend.at[0, Bh], rx_l.at[Bh], s_gx.at[0], r_gx.at[0], right)
    c_na = remote(gsend.at[0, A], rx_r.at[A], s_gx.at[1], r_gx.at[1], left)
    c_nb.start()
    c_na.start()
    image_pull(0, gi)
    image_pull(2, g2)
    c_oa.wait_recv()
    c_ob.wait_recv()
    normalize(fi[3], hi, x32.at[3], xb.at[3], sx.at[3])
    weigh(3, 1, 0, 4)
    image_pull(3, None)
    c_pa = remote(gsend.at[2, A], rx_opp.at[A], s_gx.at[2], r_gx.at[2], right)
    c_pb = remote(gsend.at[2, Bh], rx_opp.at[Bh], s_gx.at[3], r_gx.at[3], left)
    c_pa.start()
    c_pb.start()

    def text_pull(j0):
        return jnp.dot(
            wt[pl.ds(j0, 2)].reshape(2 * B, 4 * B), xb[...].reshape(4 * B, D),
            preferred_element_type=F32,
        )

    gysend[...] = text_pull(2).astype(BF16)
    c_gy = remote(gysend, gyrecv, s_gy, r_gy, sib)
    c_gy.start()
    gt[...] = text_pull(0)

    thirds = ((0, 2), (2, 3), (5, 3))

    def t_copy(slot, k):
        at = pl.ds(*thirds[k])
        return remote(tt.at[slot, at], trecv.at[at], s_t.at[k], r_t.at[k], sib)

    c_t = [t_copy(0, k) for k in range(3)]
    CH = D // 3

    def head(f_ref, d_ref, slot, sender):
        f = f_ref[...].reshape(-1, D)
        for k in range(3):
            o = lax.dot_general(
                f[:, k * CH : (k + 1) * CH], d_ref[...], TN_DIMS, preferred_element_type=F32
            ).astype(BF16)
            a = 0
            while a < CH // 16:
                b, r = divmod(k * (CH // 16) + a, RT)
                n = min(RT - r, CH // 16 - a)
                for c in range(CT):
                    tt[slot, b, pl.ds(c * RT + r, n)] = o[
                        a * 16 : (a + n) * 16, c * 128 : c * 128 + 128
                    ].reshape(n, 16, 128)
                a += n

            @pl.when(core == sender)
            def _(k=k):
                t_copy(slot, k).start()

    if TP > NT:
        zero = jnp.zeros((BLK, TP - NT, 16, 128), BF16)
        tt[0, :, pl.ds(NT, TP - NT)] = zero
        tt[1, :, pl.ds(NT, TP - NT)] = zero
    head(fi, dpp, 0, 1)
    c_gy.wait_recv()
    g = gt[...] + gyrecv[...].reshape(2 * B, D).astype(F32)
    gt[...] = g
    ysend[...] = g[B:].astype(BF16)
    dqp[...] = back(y32[...].reshape(2 * B, D), sy[...].reshape(2 * B, 1), g)
    head(ft, dqp, 1, 0)


    for k, (b0, nb) in enumerate(thirds):
        c_t[k].wait_recv()
        for kept in range(2):

            def merge_t(b, _, kept=kept):
                trecv[b] = (tt[kept, b].astype(F32) + trecv[b].astype(F32)).astype(BF16)
                return 0

            @pl.when(core == kept)
            def _(b0=b0, nb=nb, merge_t=merge_t):
                lax.fori_loop(b0, b0 + nb, merge_t, 0)

    def zpiece(d, half, r):
        return pl.ds(ZT * ((z + (r if d == 0 else NZ - r)) % NZ) + ZH * half, ZH)

    order = [[(d, 4)] + [m for r in (3, 2, 1) for m in ((1 - d, r), (d, r))] for d in range(2)]
    cz = [[None] * 7, [None] * 7]

    def z_send(d, k):
        half, r = order[d][k]
        if k < 2:
            src = trecv.at[:, zpiece(d, half, r)]
        else:
            cz[d][k - 2].wait_recv()

            def add(b, _):
                zs[d, k - 2, b] = (
                    trecv[b, zpiece(d, half, r)].astype(F32) + zr[d, k - 2, b].astype(F32)
                ).astype(BF16)
                return 0

            lax.fori_loop(0, BLK, add, 0)
            src = zs.at[d, k - 2]
        cz[d][k] = remote(src, zr.at[d, k], s_z.at[d, k], r_z.at[d, k], zpeer[1 if d == 0 else 7])
        cz[d][k].start()

    def ypiece(r, half):
        t = (yp + r) % NY
        return pl.ds(4 * (t % 2) + 2 * half, 2), pl.ds(ZN + YT * (t // 2), YT)

    cy = [[None] * 3, [None] * 3]

    def y_send(d, k):
        to = ypeer[1 if d == 0 else 3]
        half = d if k != 1 else 1 - d
        bs, ts = ypiece(2 if k == 0 else (1 if d == 0 else 3), half)
        src = trecv.at[bs, ts]
        if k == 2:
            cy[d][0].wait_recv()
            ys[d] = (trecv[bs, ts].astype(F32) + yr[d, 0].astype(F32)).astype(BF16)
            src = ys.at[d]
        cy[d][k] = remote(src, yr.at[d, k], s_yr.at[d, k], r_yr.at[d, k], to)
        cy[d][k].start()

    for k in range(2):
        for d in range(2):
            z_send(d, k)
            y_send(d, k)
    c_pa.wait_recv()
    c_pb.wait_recv()
    gsend[1] = (g2[...] + rx_opp[...].astype(F32)).astype(BF16)
    c_qa = remote(gsend.at[1, A], rx_l.at[A], s_gx.at[4], r_gx.at[4], right)
    c_qb = remote(gsend.at[1, Bh], rx_r.at[Bh], s_gx.at[5], r_gx.at[5], left)
    c_qa.start()
    c_qb.start()
    z_send(0, 2)
    z_send(1, 2)
    y_send(0, 2)
    y_send(1, 2)
    for k in (3, 4):
        z_send(0, k)
        z_send(1, k)
    for half, parts in ((0, ((0, 2), (1, 1))), (1, ((0, 1), (1, 2)))):
        bs, ts = ypiece(0, half)
        v = trecv[bs, ts].astype(F32)
        for d, k in parts:
            cy[d][k].wait_recv()
            v += yr[d, k].astype(F32)
        ysum[pl.ds(2 * half, 2)] = v.astype(BF16)
    c_x = []
    for r in range(1, NX):
        c_x.append(remote(ysum.at[(x + r) % NX], xr.at[r], s_x.at[r], r_x.at[r], xpeer[r]))
        c_x[-1].start()
    z_send(0, 5)
    z_send(1, 5)
    c_y = remote(ysend, yrecv, s_y, r_y, mate)
    c_y.start()
    z_send(0, 6)
    z_send(1, 6)
    v = ysum[x].astype(F32)
    for r in range(1, NX):
        c_x[r - 1].wait_recv()
        v += xr[r].astype(F32)
    xsum[pl.ds(0, YT)] = v.astype(BF16)
    xsum[pl.ds(YT, YW - YT)] = jnp.zeros((YW - YT, 16, 128), BF16)
    c_q = []
    for r in range(1, NZ):
        c_q.append(
            remote(xsum.at[pl.ds(YP * ((z + r) % NZ), YP)], qr.at[r], s_q.at[r], r_q.at[r], zpeer[r])
        )
        c_q[-1].start()
    for half, parts in ((0, ((0, 6), (1, 5))), (1, ((0, 5), (1, 6)))):
        for d, k in parts:
            cz[d][k].wait_recv()

        def own(b, _, half=half, parts=parts):
            v = trecv[b, zpiece(0, half, 0)].astype(F32)
            for d, k in parts:
                v += zr[d, k, b].astype(F32)
            psum[b, pl.ds(ZH * half, ZH)] = v.astype(BF16)
            return 0

        lax.fori_loop(0, BLK, own, 0)
    c_p = []
    for r in range(1, 16):
        to, blk = plane(r)
        c_p.append(remote(psum.at[blk], pr.at[r], s_p.at[r], r_p.at[r], to))
        c_p[-1].start()
    pr[0] = psum[me_plane % 8]
    v = xsum[pl.ds(YP * z, YP)].astype(F32)
    for r in range(1, NZ):
        c_q[r - 1].wait_recv()
        v += qr[r].astype(F32)
    qg[0] = v.astype(BF16)
    c_k = []
    for r in range(1, 16):
        dz, dy = r % 8, r // 8
        to = dev((z + dz) % NZ, (yp + 2 * dy) % NY, x, core)
        c_k.append(remote(qg.at[0], qg.at[r], s_k.at[r], r_k.at[r], to))
        c_k[-1].start()
    for c in c_p:
        c.wait_recv()
    total = pr[me_plane].astype(F32)
    for q in range(1, 16):
        total += pr[(me_plane + 16 - q) % 16].astype(F32)
    zg[0] = total.astype(BF16)
    c_g = []
    for r in range(1, NZ):
        c_g.append(remote(zg.at[0], zg.at[r], s_g.at[r], r_g.at[r], zpeer[r]))
        c_g[-1].start()

    outs = []

    def put(src, dst):
        outs.append(pltpu.make_async_copy(src, dst, s_out.at[len(outs)]))
        outs[-1].start()

    for c in (c_nb, c_na, c_qa, c_qb):
        c.wait_recv()
    dpf = back(x32[0], sx[0], gi[...] + rx_l[...].astype(F32) + rx_r[...].astype(F32))
    gi[...] = lax.dot_general(dpf, hi[...], NT_DIMS, preferred_element_type=F32)
    put(gi, gi_hbm)
    c_y.wait_recv()
    dqf = back(y32[0], sy[0], gt[pl.ds(0, B)] + yrecv[...].astype(F32))
    gt[pl.ds(0, B)] = lax.dot_general(dqf, ht[...], NT_DIMS, preferred_element_type=F32)
    put(gt.at[pl.ds(0, B)], gt_hbm)

    fin[pl.ds(ZN + YW * yh + YP * z, YP)] = qg[0]
    for r in range(1, 16):
        dz, dy = r % 8, r // 8
        c_k[r - 1].wait_recv()
        fin[pl.ds(ZN + YW * ((yh + dy) % 2) + YP * ((z + NZ - dz) % NZ), YP)] = qg[r]
    rest, front = pl.ds(ZN, FIN - ZN), pl.ds(0, ZN)
    c_fr = remote(fin.at[rest], finr.at[rest], s_f.at[0], r_f.at[0], sib)
    c_fr.start()
    fin[pl.ds(ZT * z, ZT)] = zg[0]
    for r in range(1, NZ):
        c_g[r - 1].wait_recv()
        fin[pl.ds(ZT * ((z + NZ - r) % NZ), ZT)] = zg[r]
    c_ff = remote(fin.at[front], finr.at[front], s_f.at[1], r_f.at[1], sib)
    c_ff.start()

    def emit(ref, out, first):
        def place_of(t):
            return t if t < ZN else ZN + YW * ((t - ZN) // YT) + (t - ZN) % YT

        r0, r1 = first // 16, -(-(first + BR // 2) // 16)
        for c in range(CT):
            r = r0
            while r < r1:
                t, n = place_of(c * RT + r), 1
                while r + n < r1 and place_of(c * RT + r + n) == t + n:
                    n += 1
                lo, up_ = max(r * 16, first), min((r + n) * 16, first + BR // 2)
                rows = ref[pl.ds(t, n)].astype(F32).reshape(n * 16, 128)
                out[pl.ds(lo - first, up_ - lo), pl.ds(c * 128, 128)] = rows[
                    lo - r * 16 : up_ - r * 16
                ]
                r += n

    @pl.when(core == 0)
    def _():
        emit(fin, wi, 0)
        c_fr.wait_recv()
        c_ff.wait_recv()
        emit(finr, wo, 0)

    @pl.when(core == 1)
    def _():
        emit(fin, wo, BR // 2)
        c_fr.wait_recv()
        c_ff.wait_recv()
        emit(finr, wi, BR // 2)

    put(wi, wi_hbm)
    put(wo, wt_hbm)
    for c in (
        [c_ra, c_rb, c_lb, c_la, c_ft, c_oa, c_ob, c_nb, c_na, c_pa, c_pb, c_qa, c_qb, c_gy, c_y]
        + c_yb + c_t + cz[0] + cz[1] + cy[0] + cy[1] + c_x + c_q + c_p + c_k + c_g + [c_fr, c_ff]
    ):
        c.wait_send()
    for c in outs:
        c.wait()


def hand_on(*refs):
    ins, outs, bufs, sem_in, sem_out = refs[:4], refs[4:8], refs[8:12], refs[12], refs[13]
    parts = []
    for a, o, v in zip(ins, outs, bufs):
        n = 4 if a.shape[0] == B else 1
        rows = a.shape[0] // n
        for k in range(n):
            at = pl.ds(k * rows, rows)
            parts.append(
                (
                    pltpu.make_async_copy(a.at[at], v.at[at], sem_in.at[len(parts)]),
                    pltpu.make_async_copy(v.at[at], o.at[at], sem_out.at[len(parts)]),
                )
            )
    for c, _ in parts:
        c.start()
    for c, d in parts:
        c.wait()
        d.start()
    for _, d in parts:
        d.wait()


def per_device(image_features, text_features, image_head, text_head):
    vm, dma = pltpu.VMEM, pltpu.SemaphoreType.DMA
    outs = (
        jax.ShapeDtypeStruct((B, D), F32),
        jax.ShapeDtypeStruct((B, D), F32),
        jax.ShapeDtypeStruct((BR // 2, D), F32),
        jax.ShapeDtypeStruct((BR // 2, D), F32),
    )
    tile = (16, 128)
    got = pl.pallas_call(
        kernel,
        out_shape=outs,
        in_specs=[pl.BlockSpec(memory_space=pl.ANY)] * 4,
        out_specs=[pl.BlockSpec(memory_space=pl.ANY)] * 4,
        scratch_shapes=[
            vm((4, B, D), BF16), vm((2, B, D), BF16), vm((D, D), BF16), vm((D, D), BF16),
            vm((4, B, D), F32), vm((4, B, D), BF16), vm((4, B, 1), F32),
            vm((2, B, D), F32), vm((4, B, D), BF16), vm((2, B, 1), F32),
            vm((4, B, 4 * B), BF16), vm((4, B, 4 * B), BF16),
            vm((B, D), F32), vm((2 * B, D), F32), vm((B, D), F32),
            vm((4 * B, D), BF16), vm((2 * B, D), BF16),
            vm((3, B, D), BF16), vm((B, D), BF16), vm((B, D), BF16), vm((B, D), BF16),
            vm((2 * B, D), BF16), vm((2 * B, D), BF16),
            vm((B, D), BF16), vm((B, D), BF16),
            vm((2, BLK, TP) + tile, BF16), vm((BLK, TP) + tile, BF16),
            vm((2, 7, BLK, ZH) + tile, BF16), vm((2, 5, BLK, ZH) + tile, BF16),
            vm((2, 3, 2, YT) + tile, BF16), vm((2, 2, YT) + tile, BF16),
            vm((4, YT) + tile, BF16), vm((4, YT) + tile, BF16),
            vm((YW,) + tile, BF16), vm((NZ, YP) + tile, BF16), vm((16, YP) + tile, BF16),
            vm((BLK, ZT) + tile, BF16), vm((16, ZT) + tile, BF16), vm((NZ, ZT) + tile, BF16),
            vm((FIN,) + tile, BF16), vm((FIN,) + tile, BF16),
            vm((BR // 2, D), F32), vm((BR // 2, D), F32),
            dma((4,)), dma((6,)), dma((6,)), dma(()), dma(()), dma((2,)), dma((2,)),
            dma((6,)), dma((6,)), dma(()), dma(()), dma(()), dma(()),
            dma((3,)), dma((3,)), dma((2, 7)), dma((2, 7)), dma((2, 3)), dma((2, 3)),
            dma((4,)), dma((4,)), dma((8,)), dma((8,)), dma((16,)), dma((16,)), dma((16,)), dma((16,)),
            dma((8,)), dma((8,)), dma((2,)), dma((2,)), dma((4,)),
        ],
        compiler_params=pltpu.CompilerParams(
            collective_id=0, has_side_effects=True, vmem_limit_bytes=63 << 20
        ),
        name="siglip_back",
    )(image_features, text_features, image_head, text_head)
    return pl.pallas_call(
        hand_on,
        out_shape=outs,
        in_specs=[pl.BlockSpec(memory_space=pl.ANY)] * 4,
        out_specs=[pl.BlockSpec(memory_space=pl.ANY)] * 4,
        scratch_shapes=[vm(o.shape, F32) for o in outs] + [dma((10,)), dma((10,))],
        name="hand_on",
    )(*got)


def solution(mesh):
    placed = (P(("cuts", "loop"), None), P(("cuts", "loop"), None), P(), P())
    return jax.shard_map(
        per_device,
        mesh=mesh,
        in_specs=placed,
        out_specs=(
            P(("cuts", "loop"), None),
            P(("cuts", "loop"), None),
            P("loop", None),
            P("loop", None),
        ),
        check_vma=False,
    )
```
